256 devices in a mesh: seq: 64 (over z, y, core), head: 4 (over x).
Axes of the slice: x: 4, y: 4, z: 8, core: 2. Of those that a mesh axis runs over, the one named last changes fastest.
Arguments:
- queries: bfloat16 [65536, 512], P('seq', 'head'), may hold values from -8 to 8
- key_rows: bfloat16 [65536, 512], P('seq', 'head'), may hold values from -8 to 8
- value_rows: bfloat16 [65536, 512], P('seq', 'head'), may hold values from -24 to 24
- offsets: int32 [4, 8], P(None, 'head'), may hold values from 0 to 7
- w_out: bfloat16 [512, 1024], P('head'), may hold values from -0.25 to 0.25
- d_out: bfloat16 [65536, 1024], P('seq', 'head'), may hold values from -6 to 6
Outputs:
- layer_out: bfloat16 [65536, 1024], P('seq', 'head')
- q_grad: bfloat16 [65536, 512], P('seq', 'head')
- k_grad: bfloat16 [65536, 512], P('seq', 'head')
- v_grad: bfloat16 [65536, 512], P('seq', 'head')
The draws below stay inside these ranges and needn't reach their ends.
Inputs may be any that keep to these rules, and one draw needn't show every extreme that they name: The offset of head h at level l is offsets[l, h] mod 2^l.
All inputs are finite; a program needn't handle non-finite values.
Results may differ from the reference program's by a relative error of at most 0.03.
Values may be sent and summed in bfloat16 or wider, within the bound.
A program may use at most 128 MiB of HBM per device.

```python
import jax
import jax.numpy as jnp
from jax import lax

D = 1024
HEADS = 8
HEAD_DIM = 64
SEG_BASE = 1024
LEVELS = 4
TOKENS = 65536
FEAT = 512


def draw_queries(key, part):
    key = jax.random.fold_in(key, 1)
    normal_rows = 1.25 * jax.random.normal(key, (TOKENS, HEADS * HEAD_DIM), jnp.float32)
    return jnp.clip(normal_rows, -7.0, 7.0).astype(jnp.bfloat16)


def draw_key_rows(key, part):
    key = jax.random.fold_in(key, 2)
    normal_rows = 1.25 * jax.random.normal(key, (TOKENS, HEADS * HEAD_DIM), jnp.float32)
    return jnp.clip(normal_rows, -7.0, 7.0).astype(jnp.bfloat16)


def touch_ends(drawn, stream_key, smallest, largest):
    dims = drawn.shape
    spot = [jax.random.randint(jax.random.fold_in(stream_key, axis), (), 0, dims[axis]) for axis in range(len(dims))]
    drawn = drawn.at[tuple(spot)].set(smallest)
    longest = dims.index(max(dims))
    spot[longest] = (spot[longest] + 1) % dims[longest]
    return drawn.at[tuple(spot)].set(largest)


def levels(rng, dims, cuts, low, high):
    gain, own = 1.0, jax.random.fold_in(rng, 6)
    for axis_at, blocks in cuts:
        steps = jnp.exp(jax.random.uniform(jax.random.fold_in(own, axis_at), (blocks,), jnp.float32, low / len(cuts), high / len(cuts)))
        gain = gain * jnp.repeat(steps, dims[axis_at] // blocks).reshape([-1 if axis == axis_at else 1 for axis in range(len(dims))])
    return gain


def centred(key, shape, scale, limit, pieces=(), dtype=jnp.bfloat16):
    array = jax.random.normal(key, shape, jnp.float32) * scale
    if len(pieces) > 0:
        array = levels(key, shape, pieces, -0.22, 0.18) * array
    return jnp.clip(array, min=-limit, max=limit).astype(dtype)


def setup_inputs(seed: int = 0) -> dict:
    keys = jax.random.split(jax.random.key(seed), 7)
    queries = draw_queries(jax.random.fold_in(keys[6], 71), 0)
    key_rows = draw_key_rows(jax.random.fold_in(keys[6], 71), 0)
    value_rows = centred(keys[2], (TOKENS, FEAT), 4.0, 24.0, ((0, 64), (1, 4)))
    offsets = touch_ends(jax.random.randint(keys[3], (LEVELS, HEADS), 0, 8), jax.random.fold_in(keys[3], 1), 0, 7).astype(jnp.int32)
    w_out = centred(keys[4], (FEAT, D), FEAT ** -0.5, 0.25, ((0, 4),))
    d_out = centred(keys[5], (TOKENS, D), 1.0, 6.0, ((0, 64), (1, 4)))
    return {"queries": queries, "key_rows": key_rows, "value_rows": value_rows, "offsets": offsets, "w_out": w_out, "d_out": d_out}


def choose_rows(source, dilation, offset):
    head_count = source.shape[1]
    shaped = source.reshape((source.shape[0] // dilation, dilation) + source.shape[1:])
    hit_mask = jnp.arange(dilation)[:, None] == (offset % dilation)[None, :]
    hit_mask = hit_mask.reshape((1, dilation, head_count) + (1,) * (source.ndim - 2))
    return jnp.sum(jnp.where(hit_mask, shaped, jnp.zeros_like(shaped)), axis=1)


def spread_rows(picked, dilation, offset, fill_value):
    head_count = picked.shape[1]
    hit_mask = jnp.arange(dilation)[:, None] == (offset % dilation)[None, :]
    hit_mask = hit_mask.reshape((1, dilation, head_count) + (1,) * (picked.ndim - 2))
    placed = jnp.where(hit_mask, jnp.expand_dims(picked, 1), fill_value)
    return placed.reshape((picked.shape[0] * dilation,) + picked.shape[1:])


def forward_segment(operands):
    query_seg, key_seg, value_seg = operands
    score_scale = HEAD_DIM ** -0.5
    score = jnp.einsum("qhd,khd->hqk", query_seg.astype(jnp.float32), key_seg.astype(jnp.float32)) * score_scale
    row_max = jnp.max(score, axis=2, keepdims=True)
    log_total = row_max + jnp.log(jnp.sum(jnp.exp(score - row_max), axis=2, keepdims=True))
    probs_b = lax.optimization_barrier(jnp.exp(score - log_total).astype(jnp.bfloat16)).astype(jnp.float32)
    level_out = jnp.einsum("hqk,khd->qhd", probs_b, value_seg.astype(jnp.float32))
    return level_out, log_total[:, :, 0].T


def backward_segment(operands):
    query_seg, key_seg, value_seg, d_seg, lse_seg, delta_seg = operands
    score_scale = HEAD_DIM ** -0.5
    score = jnp.einsum("qhd,khd->hqk", query_seg.astype(jnp.float32), key_seg.astype(jnp.float32)) * score_scale
    joint_prob = jnp.exp(score - lse_seg.T[:, :, None])
    joint_b = lax.optimization_barrier(joint_prob.astype(jnp.bfloat16)).astype(jnp.float32)
    d_prob = jnp.einsum("qhd,khd->hqk", d_seg.astype(jnp.float32), value_seg.astype(jnp.float32))
    d_score = joint_prob * (d_prob - delta_seg.T[:, :, None]) * score_scale
    d_score = lax.optimization_barrier(d_score.astype(jnp.bfloat16)).astype(jnp.float32)
    d_query = jnp.einsum("hqk,khd->qhd", d_score, key_seg.astype(jnp.float32))
    d_key = jnp.einsum("hqk,qhd->khd", d_score, query_seg.astype(jnp.float32))
    d_value = jnp.einsum("hqk,qhd->khd", joint_b, d_seg.astype(jnp.float32))
    return d_query, d_key, d_value


def reference(queries, key_rows, value_rows, offsets, w_out, d_out):
    query_3 = queries.reshape(TOKENS, HEADS, HEAD_DIM)
    key_3 = key_rows.reshape(TOKENS, HEADS, HEAD_DIM)
    value_3 = value_rows.reshape(TOKENS, HEADS, HEAD_DIM)
    level_outs = []
    level_lses = []
    segments_all = []
    for level_no in range(LEVELS):
        dilation = 2 ** level_no
        offset = offsets[level_no]
        seg_count = TOKENS // (SEG_BASE * dilation)
        segments = tuple(choose_rows(source, dilation, offset).reshape(seg_count, SEG_BASE, HEADS, HEAD_DIM) for source in (query_3, key_3, value_3))
        segments_all.append(segments)
        level_out, log_total = lax.map(forward_segment, segments)
        level_outs.append(spread_rows(level_out.reshape(TOKENS // dilation, HEADS, HEAD_DIM), dilation, offset, 0.0))
        level_lses.append(spread_rows(log_total.reshape(TOKENS // dilation, HEADS), dilation, offset, -1e30))
    lse_stack = jnp.stack(level_lses)
    row_max = jnp.max(lse_stack, axis=0)
    joint_lse = row_max + jnp.log(jnp.sum(jnp.exp(lse_stack - row_max), axis=0))
    mixture = jnp.zeros((TOKENS, HEADS, HEAD_DIM), jnp.float32)
    for level_no in range(LEVELS):
        mixture = mixture + jnp.exp(level_lses[level_no] - joint_lse)[:, :, None] * level_outs[level_no]
    attended = mixture.reshape(TOKENS, HEADS * HEAD_DIM).astype(jnp.bfloat16)
    layer_out = jnp.dot(attended, w_out, preferred_element_type=jnp.float32).astype(jnp.bfloat16)
    d_attn = jnp.dot(d_out, w_out.T, preferred_element_type=jnp.float32).astype(jnp.bfloat16)
    d_attn_3 = d_attn.reshape(TOKENS, HEADS, HEAD_DIM)
    delta_rows = jnp.sum(d_attn_3.astype(jnp.float32) * attended.reshape(TOKENS, HEADS, HEAD_DIM).astype(jnp.float32), axis=2)
    q_total = jnp.zeros((TOKENS, HEADS, HEAD_DIM), jnp.float32)
    k_total = jnp.zeros((TOKENS, HEADS, HEAD_DIM), jnp.float32)
    v_total = jnp.zeros((TOKENS, HEADS, HEAD_DIM), jnp.float32)
    for level_no in range(LEVELS):
        dilation = 2 ** level_no
        offset = offsets[level_no]
        seg_count = TOKENS // (SEG_BASE * dilation)
        query_seg, key_seg, value_seg = segments_all[level_no]
        d_seg = choose_rows(d_attn_3, dilation, offset).reshape(seg_count, SEG_BASE, HEADS, HEAD_DIM)
        lse_seg = choose_rows(joint_lse, dilation, offset).reshape(seg_count, SEG_BASE, HEADS)
        delta_seg = choose_rows(delta_rows, dilation, offset).reshape(seg_count, SEG_BASE, HEADS)
        d_query, d_key, d_value = lax.map(backward_segment, (query_seg, key_seg, value_seg, d_seg, lse_seg, delta_seg))
        n_rows = TOKENS // dilation
        q_total = q_total + spread_rows(d_query.reshape(n_rows, HEADS, HEAD_DIM), dilation, offset, 0.0)
        k_total = k_total + spread_rows(d_key.reshape(n_rows, HEADS, HEAD_DIM), dilation, offset, 0.0)
        v_total = v_total + spread_rows(d_value.reshape(n_rows, HEADS, HEAD_DIM), dilation, offset, 0.0)
    q_grad = q_total.reshape(TOKENS, HEADS * HEAD_DIM).astype(jnp.bfloat16)
    k_grad = k_total.reshape(TOKENS, HEADS * HEAD_DIM).astype(jnp.bfloat16)
    v_grad = v_total.reshape(TOKENS, HEADS * HEAD_DIM).astype(jnp.bfloat16)
    return layer_out, q_grad, k_grad, v_grad
```

```python
import functools

import jax
import jax.numpy as jnp
from jax import lax
from jax.experimental import pallas as pl
from jax.experimental.pallas import tpu as pltpu
from jax.sharding import PartitionSpec as P

MESH = pl.DeviceIdType.MESH
HD = 64
LEVELS = 4
T = 1024
C = 128
FIRST = (0, 8, 12, 14)
COUNT = (8, 4, 2, 1)
BLOCKS = 15
F32, BF16 = jnp.float32, jnp.bfloat16


def nn(a, b):
    return lax.dot_general(a, b, (((1,), (0,)), ((), ())), preferred_element_type=F32)


def nt(a, b):
    return lax.dot_general(a, b, (((1,), (1,)), ((), ())), preferred_element_type=F32)


def iota(shape, dim):
    return lax.broadcasted_iota(jnp.int32, shape, dim)


def split3(x):
    hi = x.astype(BF16)
    rest = x - hi.astype(F32)
    mid = rest.astype(BF16)
    lo = (rest - mid.astype(F32)).astype(BF16)
    return hi.astype(F32), mid.astype(F32), lo.astype(F32)


def pick_row(row, values):
    out = jnp.zeros_like(values[0] + row.astype(F32))
    for i, value in enumerate(values):
        out = jnp.where(row == i, value, out)
    return out


def kernel(
    nh,
    off,
    q_ref,
    k_ref,
    v_ref,
    w_ref,
    g_ref,
    layer_ref,
    dq_ref,
    dk_ref,
    dv_ref,
    sel1,
    sel2,
    sel3,
    qt,
    kvo,
    kvt,
    qbd,
    dbd,
    probs,
    mst,
    kvs1,
    kvs2,
    kvs3,
    wfull,
    dsend,
    drecv,
    dap,
    toko,
    tokl,
    att,
    qacc,
    dkv,
    gs1,
    gs2,
    gs3,
    gr1,
    gr2,
    gr3,
    own1,
    own2,
    own3,
    kv_ss,
    kv_rs,
    gr_ss,
    gr_rs,
    w_ss,
    w_rs,
    d_ss,
    d_rs,
    a_ss,
    a_rs,
):
    sels = (None, sel1, sel2, sel3)
    kvs = (None, kvs1, kvs2, kvs3)
    gsend = (None, gs1, gs2, gs3)
    grecv = (None, gr1, gr2, gr3)
    owns = (None, own1, own2, own3)
    seq = lax.axis_index("seq")
    hx = lax.axis_index("head")
    rank = [lax.rem(seq, 1 << l) for l in range(LEVELS)]

    def member(l, d):
        return seq - rank[l] + lax.rem(rank[l] + d, 1 << l)

    def slot(l, d):
        return (1 << l) - 2 - l + 1 + d - 1 if l else 0

    def head_peer(d):
        return lax.rem(hx + d, nh)

    barrier = pltpu.get_barrier_semaphore()
    for d in range(1, 8):
        pl.semaphore_signal(barrier, inc=1, device_id=(member(3, d), hx), device_id_type=MESH)
    for d in range(1, nh):
        pl.semaphore_signal(barrier, inc=1, device_id=(seq, head_peer(d)), device_id_type=MESH)
    pl.semaphore_wait(barrier, 7 + nh - 1)

    def w_copy(d):
        return pltpu.make_async_remote_copy(
            src_ref=w_ref.at[:, pl.ds(pl.multiple_of(head_peer(d) * 256, 256), 256)],
            dst_ref=wfull.at[pl.ds(pl.multiple_of(hx * 128, 128), 128), :],
            send_sem=w_ss.at[d - 1],
            recv_sem=w_rs.at[d - 1],
            device_id=(seq, head_peer(d)),
            device_id_type=MESH,
        )

    for d in range(1, nh):
        w_copy(d).start()
    own_w = pl.ds(pl.multiple_of(hx * 128, 128), 128)
    wfull[own_w, :] = w_ref[:, pl.ds(pl.multiple_of(hx * 256, 256), 256)]

    lane = iota((1, 256), 1)
    second = lane >= C
    offs = [[lax.rem(off[l, h], 1 << l) for h in range(2)] for l in range(LEVELS)]

    def kv_copy(l, d):
        n = T >> l
        i = slot(l, d)
        return pltpu.make_async_remote_copy(
            src_ref=kvs[l],
            dst_ref=kvo.at[l, pl.ds(pl.multiple_of(rank[l] * n, n), n), pl.ds(0, 256)],
            send_sem=kv_ss.at[i],
            recv_sem=kv_rs.at[i],
            device_id=(member(l, d), hx),
            device_id_type=MESH,
        )

    kv0 = jnp.concatenate([k_ref[...], v_ref[...]], axis=1)
    kvo[0, :, 0:256] = kv0
    kvo[:, :, 256:384] = jnp.ones((LEVELS, T, 128), BF16)
    kv_head1 = lax.rem(iota((C, 256), 1), 128) >= HD
    for l in (1, 2, 3):
        r = 1 << l
        tok = C * r
        n = T >> l
        row2 = iota((256, tok), 0)
        target = lax.rem(row2, C) * r + jnp.where(row2 >= C, offs[l][1], offs[l][0])
        selt = jnp.where(iota((256, tok), 1) == target, 1.0, 0.0).astype(BF16)
        for c in range(COUNT[l]):
            both = nn(selt, kvo[0, c * tok : (c + 1) * tok, 0:256])
            kvs[l][c * C : (c + 1) * C, :] = jnp.where(kv_head1, both[C:], both[:C]).astype(BF16)
        for d in range(1, r):
            kv_copy(l, d).start()
        kvo[l, pl.ds(pl.multiple_of(rank[l] * n, n), n), 0:256] = kvs[l][...]
        target = lax.rem(lane, C) * r + jnp.where(second, offs[l][1], offs[l][0])
        sels[l][...] = jnp.where(iota((tok, 256), 0) == target, 1.0, 0.0).astype(BF16)

    eye = jnp.where(iota((256, 256), 0) == iota((256, 256), 1), 1.0, 0.0).astype(BF16)
    diag = (iota((C, 256), 0) >= HD) == (iota((C, 256), 1) >= C)
    qt[...] = (nt(eye[:C, :C], q_ref[...]) * 0.125).astype(BF16)
    for l in range(LEVELS):
        tok = C << l
        for c in range(COUNT[l]):
            part = qt[:, c * tok : (c + 1) * tok]
            if l == 0:
                both = jnp.concatenate([part, part], axis=1).astype(F32)
            else:
                both = nn(part, sels[l][...])
            qbd[FIRST[l] + c] = jnp.where(diag, both, 0.0).astype(BF16)
    dbd[:, 144:256, :] = jnp.zeros((BLOCKS, 112, 256), BF16)
    kvt[:, 256:272, :] = jnp.ones((LEVELS, 16, T), BF16)

    row16 = iota((16, 256), 0)
    own_row = lax.div(row16, 3) == lax.div(iota((16, 256), 1), C)
    top = iota((C, C), 0) < HD

    def transpose_kv(l):
        for c in range(4):
            rows = slice(c * 256, (c + 1) * 256)
            kvt[l, 0:256, rows] = nt(eye, kvo[l, rows, 0:256]).astype(BF16)

    def forward_block(l, c):
        b = FIRST[l] + c
        score = nn(kvo[l, :, 0:128], qbd[b])
        top_score = jnp.max(score, axis=0, keepdims=True)
        prob = jnp.exp(score - top_score).astype(BF16)
        probs[b] = prob
        out = nn(kvt[l, 128:272, :], prob)
        total = out[C : C + 1]
        lse = top_score + jnp.log(total)
        mst[b, 0:1, :] = top_score
        out = out[:C] * (1.0 / total)
        if l == 0:
            where = pl.ds(pl.multiple_of(c * C, C), C)
            toko[0, :, where] = jnp.where(top, out[:, :C], out[:, C:])
            tokl[0, 0:1, where] = lse[:, :C]
            tokl[0, 1:2, where] = lse[:, C:]
            return
        r = 1 << l
        tok = C * r
        where = pl.ds(pl.multiple_of(c * tok, tok), tok)
        pieces = pick_row(lax.rem(row16, 3), split3(lse))
        pieces = jnp.where(own_row, pieces, 0.0)
        packed = jnp.concatenate([jnp.where(diag, out, 0.0), pieces], axis=0).astype(BF16)
        placed = nt(packed, sels[l][...])
        toko[l, :, where] = placed[:C]
        phase = lax.rem(iota((1, tok), 1), r)
        for h in range(2):
            i = C + 3 * h
            value = placed[i : i + 1] + placed[i + 1 : i + 2] + placed[i + 2 : i + 3]
            tokl[l, h : h + 1, where] = jnp.where(phase == offs[l][h], value, -1e30)

    def forward_level(l, first, last):
        if last - first == 1:
            forward_block(l, first)
        else:
            pl.loop(first, last)(lambda c: forward_block(l, c))

    def d_copy(d):
        return pltpu.make_async_remote_copy(
            src_ref=dsend.at[pl.ds(pl.multiple_of(head_peer(d) * 128, 128), 128), :],
            dst_ref=drecv.at[d - 1],
            send_sem=d_ss.at[d - 1],
            recv_sem=d_rs.at[d - 1],
            device_id=(seq, head_peer(d)),
            device_id_type=MESH,
        )

    transpose_kv(0)
    forward_level(0, 0, 4)
    for d in range(1, nh):
        w_copy(d).wait_recv()
    for c in range(4):
        cols = slice(c * 256, (c + 1) * 256)
        dsend[:, cols] = nt(wfull[...], g_ref[cols, :]).astype(BF16)
    for d in range(1, nh):
        d_copy(d).start()
    forward_level(0, 4, 8)
    for l in (1, 2, 3):
        for d in range(1, 1 << l):
            kv_copy(l, d).wait_recv()
        transpose_kv(l)
        forward_level(l, 0, COUNT[l])

    lses = [tokl[l, 0:2, :] for l in range(LEVELS)]
    peak = jnp.maximum(jnp.maximum(lses[0], lses[1]), jnp.maximum(lses[2], lses[3]))
    total = sum(jnp.exp(x - peak) for x in lses)
    joint = peak + jnp.log(total)
    is_top = iota((C, T), 0) < HD
    mixed = jnp.zeros((C, T), F32)
    for l in range(LEVELS):
        weight = jnp.exp(lses[l] - joint)
        mixed = mixed + jnp.where(is_top, weight[0:1], weight[1:2]) * toko[l]
    mixed_b = mixed.astype(BF16)
    dap[128:256, :] = mixed_b
    own_cols = pl.ds(pl.multiple_of(hx * 128, 128), 128)
    att[:, own_cols] = mixed_b.astype(F32).T.astype(BF16)
    rowt = iota((16, T), 0)
    hi, mid, lo = split3(joint)
    dap[256:272, :] = pick_row(
        rowt, (hi[0:1], mid[0:1], lo[0:1], hi[1:2], mid[1:2], lo[1:2])
    ).astype(BF16)

    def a_copy(d):
        return pltpu.make_async_remote_copy(
            src_ref=att.at[:, own_cols],
            dst_ref=att.at[:, own_cols],
            send_sem=a_ss.at[d - 1],
            recv_sem=a_rs.at[d - 1],
            device_id=(seq, head_peer(d)),
            device_id_type=MESH,
        )

    for d in range(1, nh):
        a_copy(d).start()

    d_sum = dsend[pl.ds(pl.multiple_of(hx * 128, 128), 128), :].astype(F32)
    for d in range(1, nh):
        d_copy(d).wait_recv()
        d_sum = d_sum + drecv[d - 1].astype(F32)
    dap[0:128, :] = d_sum.astype(BF16)

    def prepare(l, c):
        b = FIRST[l] + c
        tok = C << l
        part = dap[:, c * tok : (c + 1) * tok]
        if l == 0:
            both = jnp.concatenate([part, part], axis=1).astype(F32)
        else:
            both = nn(part, sels[l][...])
        x = both[256:272]
        lse = jnp.where(second, x[3:4] + x[4:5] + x[5:6], x[0:1] + x[1:2] + x[2:3])
        coef = jnp.exp(mst[b, 0:1, :] - lse)
        d_b = jnp.where(diag, both[0:128] * coef, 0.0).astype(BF16)
        dbd[b, 0:128, :] = d_b
        delta = jnp.sum(d_b.astype(F32) * both[128:256], axis=0, keepdims=True)
        dbd[b, 128:144, :] = pick_row(row16, [-x for x in split3(delta)]).astype(BF16)

    def backward_block(l, c, fresh):
        b = FIRST[l] + c
        prob = probs[b]
        d_prob = nn(kvo[l, :, 128:384], dbd[b])
        d_score = prob * d_prob.astype(BF16)
        d_q = nn(kvt[l, 0:128, :], d_score) * 0.125
        d_k = nt(d_score, qbd[b])
        d_v = nt(prob, dbd[b, 0:128, :])
        if fresh:
            dkv[:, 0:128] = d_k
            dkv[:, 128:256] = d_v
        else:
            dkv[:, 0:128] += d_k
            dkv[:, 128:256] += d_v
        if l == 0:
            where = pl.ds(pl.multiple_of(c * C, C), C)
            qacc[where, :] += jnp.where(top, d_q[:, :C], d_q[:, C:]).T
        else:
            tok = C << l
            placed = nt(sels[l][...], jnp.where(diag, d_q, 0.0).astype(BF16))
            if l == 3:
                qacc[...] = placed
            else:
                qacc[pl.ds(pl.multiple_of(c * tok, tok), tok), :] += placed

    def g_copy(l, d):
        n = T >> l
        i = slot(l, d)
        part = lax.rem(rank[l] + d, 1 << l)
        return pltpu.make_async_remote_copy(
            src_ref=gsend[l].at[pl.ds(pl.multiple_of(part * n, n), n), :],
            dst_ref=grecv[l].at[d - 1],
            send_sem=gr_ss.at[i],
            recv_sem=gr_rs.at[i],
            device_id=(member(l, d), hx),
            device_id_type=MESH,
        )

    for l in (3, 2, 1, 0):
        for c in range(COUNT[l]):
            prepare(l, c)
        backward_block(l, 0, True)
        if COUNT[l] > 1:
            pl.loop(1, COUNT[l])(lambda c: backward_block(l, c, False))
        if l:
            n = T >> l
            gsend[l][...] = dkv[...].astype(BF16)
            for d in range(1, 1 << l):
                g_copy(l, d).start()
            owns[l][...] = dkv[pl.ds(pl.multiple_of(rank[l] * n, n), n), :]

    dq_ref[...] = qacc[...].astype(BF16)

    for d in range(1, nh):
        a_copy(d).wait_recv()
    layer_ref[...] = nn(att[...], wfull[...]).astype(BF16)

    for l in (3, 2, 1):
        tok = C << l
        for d in range(1, 1 << l):
            g_copy(l, d).wait_recv()
        for c in range(COUNT[l]):
            rows = slice(c * C, (c + 1) * C)
            grad = owns[l][rows, :]
            for d in range(1, 1 << l):
                grad = grad + grecv[l][d - 1, rows, :].astype(F32)
            stacked = jnp.concatenate(
                [jnp.where(kv_head1, 0.0, grad), jnp.where(kv_head1, grad, 0.0)], axis=0
            ).astype(BF16)
            dkv[c * tok : (c + 1) * tok, :] += nn(sels[l][...], stacked)
    dk_ref[...] = dkv[:, 0:128].astype(BF16)
    dv_ref[...] = dkv[:, 128:256].astype(BF16)

    for d in range(1, nh):
        w_copy(d).wait_send()
        d_copy(d).wait_send()
        a_copy(d).wait_send()
    for l in (1, 2, 3):
        for d in range(1, 1 << l):
            kv_copy(l, d).wait_send()
            g_copy(l, d).wait_send()


def shards(nh, queries, key_rows, value_rows, offsets, w_out, d_out):
    vmem = pl.BlockSpec(memory_space=pltpu.VMEM)
    dma = pltpu.SemaphoreType.DMA
    feat = 128 * nh
    level_bf16 = [pltpu.VMEM((T >> l, 256), BF16) for l in (1, 2, 3)]
    scratch = [
        *[pltpu.VMEM((C << l, 256), BF16) for l in (1, 2, 3)],
        pltpu.VMEM((128, T), BF16),
        pltpu.VMEM((LEVELS, T, 384), BF16),
        pltpu.VMEM((LEVELS, 272, T), BF16),
        pltpu.VMEM((BLOCKS, 128, 256), BF16),
        pltpu.VMEM((BLOCKS, 256, 256), BF16),
        pltpu.VMEM((BLOCKS, T, 256), BF16),
        pltpu.VMEM((BLOCKS, 8, 256), F32),
        *level_bf16,
        pltpu.VMEM((feat, 256), BF16),
        pltpu.VMEM((feat, T), BF16),
        pltpu.VMEM((max(nh - 1, 1), 128, T), BF16),
        pltpu.VMEM((272, T), BF16),
        pltpu.VMEM((LEVELS, 128, T), F32),
        pltpu.VMEM((LEVELS, 8, T), F32),
        pltpu.VMEM((T, feat), BF16),
        pltpu.VMEM((T, 128), F32),
        pltpu.VMEM((T, 256), F32),
        *[pltpu.VMEM((T, 256), BF16) for l in (1, 2, 3)],
        *[pltpu.VMEM(((1 << l) - 1, T >> l, 256), BF16) for l in (1, 2, 3)],
        *[pltpu.VMEM((T >> l, 256), F32) for l in (1, 2, 3)],
        dma((11,)),
        dma((11,)),
        dma((11,)),
        dma((11,)),
        *[dma((max(nh - 1, 1),))] * 6,
    ]
    return pl.pallas_call(
        functools.partial(kernel, nh),
        out_shape=(
            jax.ShapeDtypeStruct((T, 256), BF16),
            jax.ShapeDtypeStruct((T, 128), BF16),
            jax.ShapeDtypeStruct((T, 128), BF16),
            jax.ShapeDtypeStruct((T, 128), BF16),
        ),
        in_specs=[pl.BlockSpec(memory_space=pltpu.SMEM)] + [vmem] * 5,
        out_specs=(vmem,) * 4,
        scratch_shapes=scratch,
        compiler_params=pltpu.CompilerParams(
            collective_id=0, has_side_effects=True, vmem_limit_bytes=56 * 1024 * 1024
        ),
        cost_estimate=pl.CostEstimate(flops=4_000_000_000, bytes_accessed=3_000_000, transcendentals=4_000_000),
    )(offsets, queries, key_rows, value_rows, w_out, d_out)


def solution(mesh):
    in_specs = (
        P("seq", "head"),
        P("seq", "head"),
        P("seq", "head"),
        P(None, "head"),
        P("head", None),
        P("seq", "head"),
    )
    out_specs = (P("seq", "head"), P("seq", "head"), P("seq", "head"), P("seq", "head"))
    return jax.shard_map(
        functools.partial(shards, mesh.shape["head"]),
        mesh=mesh,
        in_specs=in_specs,
        out_specs=out_specs,
        check_vma=False,
    )
```

```python
import functools

import jax
import jax.numpy as jnp
from jax import lax
from jax.experimental import pallas as pl
from jax.experimental.pallas import tpu as pltpu
from jax.sharding import PartitionSpec as P

MESH = pl.DeviceIdType.MESH
HD = 64
LEVELS = 4
T = 1024
C = 128
FIRST = (0, 8, 12, 14)
COUNT = (8, 4, 2, 1)
BLOCKS = 15
F32, BF16 = jnp.float32, jnp.bfloat16


def nn(a, b):
    return lax.dot_general(a, b, (((1,), (0,)), ((), ())), preferred_element_type=F32)


def nt(a, b):
    return lax.dot_general(a, b, (((1,), (1,)), ((), ())), preferred_element_type=F32)


def iota(shape, dim):
    return lax.broadcasted_iota(jnp.int32, shape, dim)


def split3(x):
    hi = x.astype(BF16)
    rest = x - hi.astype(F32)
    mid = rest.astype(BF16)
    lo = (rest - mid.astype(F32)).astype(BF16)
    return hi.astype(F32), mid.astype(F32), lo.astype(F32)


def pick_row(row, values):
    out = jnp.zeros_like(values[0] + row.astype(F32))
    for i, value in enumerate(values):
        out = jnp.where(row == i, value, out)
    return out


def kernel(
    nh,
    off,
    q_ref,
    k_ref,
    v_ref,
    w_ref,
    g_ref,
    layer_ref,
    dq_ref,
    dk_ref,
    dv_ref,
    sel1,
    sel2,
    sel3,
    qt,
    kv1,
    kv2,
    kv3,
    kvt,
    qbd,
    dbd,
    probs,
    grads,
    scores,
    kvs1,
    kvs2,
    kvs3,
    wfull,
    dsend,
    drecv,
    dap,
    toko,
    tokl,
    att,
    dkv,
    dqs,
    gs1,
    gs2,
    gs3,
    gr1,
    gr2,
    gr3,
    own1,
    own2,
    own3,
    stk1,
    stk2,
    stk3,
    kv_ss,
    kv_rs,
    gr_ss,
    gr_rs,
    w_ss,
    w_rs,
    d_ss,
    d_rs,
    a_ss,
    a_rs,
):
    sels = (None, sel1, sel2, sel3)
    kvs = (None, kvs1, kvs2, kvs3)
    kv = (None, kv1, kv2, kv3)
    gsend = (None, gs1, gs2, gs3)
    grecv = (None, gr1, gr2, gr3)
    owns = (None, own1, own2, own3)
    stacks = (None, stk1, stk2, stk3)
    seq = lax.axis_index("seq")
    hx = lax.axis_index("head")
    rank = [lax.rem(seq, 1 << l) for l in range(LEVELS)]

    def member(l, d):
        return seq - rank[l] + lax.rem(rank[l] + d, 1 << l)

    def slot(l, d):
        return (1 << l) - 2 - l + d if l else 0

    def head_peer(d):
        return lax.rem(hx + d, nh)

    def keys(l):
        return k_ref[...] if l == 0 else kv[l][:, 0:128]

    def values(l):
        return v_ref[...] if l == 0 else kv[l][:, 128:256]

    barrier = pltpu.get_barrier_semaphore()
    for d in range(1, 8):
        pl.semaphore_signal(barrier, inc=1, device_id=(member(3, d), hx), device_id_type=MESH)
    for d in range(1, nh):
        pl.semaphore_signal(barrier, inc=1, device_id=(seq, head_peer(d)), device_id_type=MESH)
    pl.semaphore_wait(barrier, 7 + nh - 1)

    own_rows = pl.ds(pl.multiple_of(hx * 128, 128), 128)

    def w_copy(d):
        return pltpu.make_async_remote_copy(
            src_ref=w_ref.at[:, pl.ds(pl.multiple_of(head_peer(d) * 256, 256), 256)],
            dst_ref=wfull.at[own_rows, :],
            send_sem=w_ss.at[d - 1],
            recv_sem=w_rs.at[d - 1],
            device_id=(seq, head_peer(d)),
            device_id_type=MESH,
        )

    for d in range(1, nh):
        w_copy(d).start()
    wfull[own_rows, :] = w_ref[:, pl.ds(pl.multiple_of(hx * 256, 256), 256)]

    lane = iota((1, 256), 1)
    second = lane >= C
    offs = [[lax.rem(off[l, h], 1 << l) for h in range(2)] for l in range(LEVELS)]

    def kv_copy(l, d):
        n = T >> l
        i = slot(l, d)
        return pltpu.make_async_remote_copy(
            src_ref=kvs[l],
            dst_ref=kv[l].at[pl.ds(pl.multiple_of(rank[l] * n, n), n), :],
            send_sem=kv_ss.at[i],
            recv_sem=kv_rs.at[i],
            device_id=(member(l, d), hx),
            device_id_type=MESH,
        )

    kv_head1 = lax.rem(iota((C, 256), 1), 128) >= HD
    for l in (3, 2, 1):
        r = 1 << l
        tok = C * r
        n = T >> l
        row2 = iota((256, tok), 0)
        target = lax.rem(row2, C) * r + jnp.where(row2 >= C, offs[l][1], offs[l][0])
        selt = jnp.where(iota((256, tok), 1) == target, 1.0, 0.0).astype(BF16)
        for c in range(COUNT[l]):
            rows = slice(c * tok, (c + 1) * tok)
            both = nn(selt, jnp.concatenate([k_ref[rows, :], v_ref[rows, :]], axis=1))
            kvs[l][c * C : (c + 1) * C, :] = jnp.where(kv_head1, both[C:], both[:C]).astype(BF16)
        for d in range(1, r):
            kv_copy(l, d).start()
        kv[l][pl.ds(pl.multiple_of(rank[l] * n, n), n), :] = kvs[l][...]

    eye = jnp.where(iota((256, 256), 0) == iota((256, 256), 1), 1.0, 0.0).astype(BF16)
    diag = (iota((C, 256), 0) >= HD) == (iota((C, 256), 1) >= C)
    row16 = iota((16, 256), 0)
    own_row = lax.div(row16, 3) == lax.div(iota((16, 256), 1), C)
    top = iota((C, C), 0) < HD
    ones16 = jnp.ones((16, T), BF16)
    ones128 = jnp.ones((T, 128), BF16)
    zeros112 = jnp.zeros((112, 256), BF16)

    qt[...] = (nt(eye[:C, :C], q_ref[...]) * 0.125).astype(BF16)

    def place_queries(l):
        tok = C << l
        if l:
            target = lax.rem(lane, C) * (1 << l) + jnp.where(second, offs[l][1], offs[l][0])
            sels[l][...] = jnp.where(iota((tok, 256), 0) == target, 1.0, 0.0).astype(BF16)
        for c in range(COUNT[l]):
            part = qt[:, c * tok : (c + 1) * tok]
            if l == 0:
                both = jnp.concatenate([part, part], axis=1).astype(F32)
            else:
                both = nn(part, sels[l][...])
            qbd[FIRST[l] + c] = jnp.where(diag, both, 0.0).astype(BF16)

    def transpose_kv(l):
        for c in range(4):
            rows = slice(c * 256, (c + 1) * 256)
            if l == 0:
                part = jnp.concatenate([k_ref[rows, :], v_ref[rows, :]], axis=1)
            else:
                part = kv[l][rows, :]
            kvt[l, :, rows] = nt(eye, part).astype(BF16)

    where = [(l, c) for l in range(LEVELS) for c in range(COUNT[l])]
    top_scores = {}

    def score_stage(b):
        l, c = where[b]
        score = nn(keys(l), qbd[b])
        scores[b % 2] = score
        top_scores[b] = jnp.max(score, axis=0, keepdims=True)

    def prob_stage(b):
        probs[b] = jnp.exp(scores[b % 2] - top_scores[b]).astype(BF16)

    def out_stage(b):
        l, c = where[b]
        out = nn(jnp.concatenate([kvt[l, 128:256, :], ones16], axis=0), probs[b])
        total = out[C : C + 1]
        lse = top_scores[b] + jnp.log(total)
        out = out[:C] * (1.0 / total)
        if l == 0:
            cols = slice(c * C, (c + 1) * C)
            toko[0, :, cols] = jnp.where(top, out[:, :C], out[:, C:])
            tokl[0, 0:1, cols] = lse[:, :C]
            tokl[0, 1:2, cols] = lse[:, C:]
            return
        r = 1 << l
        tok = C * r
        cols = slice(c * tok, (c + 1) * tok)
        pieces = pick_row(lax.rem(row16, 3), split3(lse))
        pieces = jnp.where(own_row, pieces, 0.0)
        packed = jnp.concatenate([jnp.where(diag, out, 0.0), pieces], axis=0).astype(BF16)
        placed = nt(packed, sels[l][...])
        toko[l, :, cols] = placed[:C]
        phase = lax.rem(iota((1, tok), 1), r)
        for h in range(2):
            i = C + 3 * h
            value = placed[i : i + 1] + placed[i + 1 : i + 2] + placed[i + 2 : i + 3]
            tokl[l, h : h + 1, cols] = jnp.where(phase == offs[l][h], value, -1e30)

    def d_copy(d):
        return pltpu.make_async_remote_copy(
            src_ref=dsend.at[pl.ds(pl.multiple_of(head_peer(d) * 128, 128), 128), :],
            dst_ref=drecv.at[d - 1],
            send_sem=d_ss.at[d - 1],
            recv_sem=d_rs.at[d - 1],
            device_id=(seq, head_peer(d)),
            device_id_type=MESH,
        )

    place_queries(0)
    for step in range(BLOCKS + 2):
        if step == 4:
            for d in range(1, nh):
                w_copy(d).wait_recv()
            for c in range(4):
                cols = slice(c * 256, (c + 1) * 256)
                dsend[:, cols] = nt(wfull[...], g_ref[cols, :]).astype(BF16)
            for d in range(1, nh):
                d_copy(d).start()
        if step in FIRST[1:]:
            l = FIRST.index(step)
            for d in range(1, 1 << l):
                kv_copy(l, d).wait_recv()
            transpose_kv(l)
        if step < BLOCKS:
            score_stage(step)
        if step == 0:
            transpose_kv(0)
        if step in (1, 2, 3):
            place_queries(step)
        if 0 <= step - 1 < BLOCKS:
            prob_stage(step - 1)
        if 0 <= step - 2:
            out_stage(step - 2)

    lses = [tokl[l, 0:2, :] for l in range(LEVELS)]
    peak = jnp.maximum(jnp.maximum(lses[0], lses[1]), jnp.maximum(lses[2], lses[3]))
    total = sum(jnp.exp(x - peak) for x in lses)
    joint = peak + jnp.log(total)
    is_top = iota((C, T), 0) < HD
    mixed = jnp.zeros((C, T), F32)
    for l in range(LEVELS):
        weight = jnp.exp(lses[l] - joint)
        mixed = mixed + jnp.where(is_top, weight[0:1], weight[1:2]) * toko[l]
    mixed_b = mixed.astype(BF16)
    dap[128:256, :] = mixed_b
    att[:, own_rows] = mixed_b.astype(F32).T.astype(BF16)

    def a_copy(d):
        return pltpu.make_async_remote_copy(
            src_ref=att.at[:, own_rows],
            dst_ref=att.at[:, own_rows],
            send_sem=a_ss.at[d - 1],
            recv_sem=a_rs.at[d - 1],
            device_id=(seq, head_peer(d)),
            device_id_type=MESH,
        )

    for d in range(1, nh):
        a_copy(d).start()

    rowt = iota((16, T), 0)
    hi, mid, lo = split3(joint)
    dap[256:272, :] = pick_row(
        rowt, (hi[0:1], mid[0:1], lo[0:1], hi[1:2], mid[1:2], lo[1:2])
    ).astype(BF16)

    for d in range(1, nh):
        d_copy(d).wait_recv()
    d_sum = dsend[own_rows, :].astype(F32)
    for d in range(1, nh):
        d_sum = d_sum + drecv[d - 1].astype(F32)
    dap[0:128, :] = d_sum.astype(BF16)

    def prepare(b):
        l, c = where[b]
        tok = C << l
        part = dap[:, c * tok : (c + 1) * tok]
        if l == 0:
            both = jnp.concatenate([part, part], axis=1).astype(F32)
        else:
            both = nn(part, sels[l][...])
        x = both[256:272]
        lse = jnp.where(second, x[3:4] + x[4:5] + x[5:6], x[0:1] + x[1:2] + x[2:3])
        coef = jnp.exp(top_scores[b] - lse)
        d_b = jnp.where(diag, both[0:128] * coef, 0.0).astype(BF16)
        dbd[b, 0:128, :] = d_b
        delta = jnp.sum(d_b.astype(F32) * both[128:256], axis=0, keepdims=True)
        dbd[b, 128:144, :] = pick_row(row16, [-x for x in split3(delta)]).astype(BF16)

    def grad_stage(b):
        l, c = where[b]
        d_prob = nn(
            jnp.concatenate([values(l), ones128], axis=1),
            jnp.concatenate([dbd[b], zeros112], axis=0),
        )
        grads[b] = probs[b] * d_prob.astype(BF16)

    def query_stage(b):
        l, c = where[b]
        d_q = nn(kvt[l, 0:128, :], grads[b]) * 0.125
        if l == 0:
            dqs[b] = jnp.where(top, d_q[:, :C], d_q[:, C:]).T
        else:
            qbd[b] = jnp.where(diag, d_q, 0.0).astype(BF16)

    def side(refs):
        return jnp.concatenate(refs, axis=1)

    def key_stage(blocks, fresh):
        d_k = nt(side([grads[b] for b in blocks]), side([qbd[b] for b in blocks]))
        d_v = nt(side([probs[b] for b in blocks]), side([dbd[b, 0:128, :] for b in blocks]))
        if fresh:
            dkv[:, 0:128] = d_k
            dkv[:, 128:256] = d_v
        else:
            dkv[:, 0:128] += d_k
            dkv[:, 128:256] += d_v

    def g_copy(l, d):
        n = T >> l
        i = slot(l, d)
        part = lax.rem(rank[l] + d, 1 << l)
        return pltpu.make_async_remote_copy(
            src_ref=gsend[l].at[pl.ds(pl.multiple_of(part * n, n), n), :],
            dst_ref=grecv[l].at[d - 1],
            send_sem=gr_ss.at[i],
            recv_sem=gr_rs.at[i],
            device_id=(member(l, d), hx),
            device_id_type=MESH,
        )

    groups = [[14], [12, 13], [8, 9, 10, 11], [0, 1, 2, 3], [4, 5, 6, 7]]
    for b in groups[0]:
        prepare(b)
        grad_stage(b)
    for i, group in enumerate(groups):
        if i + 1 < len(groups):
            for b in groups[i + 1]:
                prepare(b)
                grad_stage(b)
        key_stage(group, group[0] != 4)
        for b in group:
            query_stage(b)
        l = where[group[0]][0]
        if l:
            n = T >> l
            gsend[l][...] = dkv[...].astype(BF16)
            for d in range(1, 1 << l):
                g_copy(l, d).start()
            owns[l][...] = dkv[pl.ds(pl.multiple_of(rank[l] * n, n), n), :]

    for d in range(1, nh):
        a_copy(d).wait_recv()
    layer_ref[...] = nn(att[...], wfull[...]).astype(BF16)

    for l in (3, 2, 1):
        for d in range(1, 1 << l):
            g_copy(l, d).wait_recv()
    for l in (3, 2, 1):
        for c in range(COUNT[l]):
            rows = slice(c * C, (c + 1) * C)
            grad = owns[l][rows, :]
            for d in range(1, 1 << l):
                grad = grad + grecv[l][d - 1, rows, :].astype(F32)
            stacks[l][c, 0:C, :] = jnp.where(kv_head1, 0.0, grad).astype(BF16)
            stacks[l][c, C:256, :] = jnp.where(kv_head1, grad, 0.0).astype(BF16)
    for c in range(4):
        rows = slice(c * 256, (c + 1) * 256)
        place = side([sel1[...], sel2[c % 2 * 256 : c % 2 * 256 + 256, :], sel3[rows, :]])
        d_q = nt(place, side([qbd[8 + c], qbd[12 + c // 2], qbd[14]]))
        for half in range(2):
            part = slice(half * C, half * C + C)
            d_rows = slice(c * 256 + half * C, c * 256 + half * C + C)
            dq_ref[d_rows, :] = (d_q[part] + dqs[2 * c + half]).astype(BF16)
        d_kv = dkv[rows, :] + nn(
            place, jnp.concatenate([stk1[c], stk2[c // 2], stk3[0]], axis=0)
        )
        dk_ref[rows, :] = d_kv[:, 0:128].astype(BF16)
        dv_ref[rows, :] = d_kv[:, 128:256].astype(BF16)

    for d in range(1, nh):
        w_copy(d).wait_send()
        d_copy(d).wait_send()
        a_copy(d).wait_send()
    for l in (1, 2, 3):
        for d in range(1, 1 << l):
            kv_copy(l, d).wait_send()
            g_copy(l, d).wait_send()


def shards(nh, queries, key_rows, value_rows, offsets, w_out, d_out):
    vmem = pl.BlockSpec(memory_space=pltpu.VMEM)
    dma = pltpu.SemaphoreType.DMA
    feat = 128 * nh
    scratch = [
        *[pltpu.VMEM((C << l, 256), BF16) for l in (1, 2, 3)],
        pltpu.VMEM((128, T), BF16),
        *[pltpu.VMEM((T, 256), BF16) for l in (1, 2, 3)],
        pltpu.VMEM((LEVELS, 256, T), BF16),
        pltpu.VMEM((BLOCKS, 128, 256), BF16),
        pltpu.VMEM((BLOCKS, 144, 256), BF16),
        pltpu.VMEM((BLOCKS, T, 256), BF16),
        pltpu.VMEM((BLOCKS, T, 256), BF16),
        pltpu.VMEM((2, T, 256), F32),
        *[pltpu.VMEM((T >> l, 256), BF16) for l in (1, 2, 3)],
        pltpu.VMEM((feat, 256), BF16),
        pltpu.VMEM((feat, T), BF16),
        pltpu.VMEM((max(nh - 1, 1), 128, T), BF16),
        pltpu.VMEM((272, T), BF16),
        pltpu.VMEM((LEVELS, 128, T), F32),
        pltpu.VMEM((LEVELS, 8, T), F32),
        pltpu.VMEM((T, feat), BF16),
        pltpu.VMEM((T, 256), F32),
        pltpu.VMEM((8, C, 128), F32),
        *[pltpu.VMEM((T, 256), BF16) for l in (1, 2, 3)],
        *[pltpu.VMEM(((1 << l) - 1, T >> l, 256), BF16) for l in (1, 2, 3)],
        *[pltpu.VMEM((T >> l, 256), F32) for l in (1, 2, 3)],
        *[pltpu.VMEM((COUNT[l], 256, 256), BF16) for l in (1, 2, 3)],
        dma((11,)),
        dma((11,)),
        dma((11,)),
        dma((11,)),
        *[dma((max(nh - 1, 1),))] * 6,
    ]
    return pl.pallas_call(
        functools.partial(kernel, nh),
        out_shape=(
            jax.ShapeDtypeStruct((T, 256), BF16),
            jax.ShapeDtypeStruct((T, 128), BF16),
            jax.ShapeDtypeStruct((T, 128), BF16),
            jax.ShapeDtypeStruct((T, 128), BF16),
        ),
        in_specs=[pl.BlockSpec(memory_space=pltpu.SMEM)] + [vmem] * 5,
        out_specs=(vmem,) * 4,
        scratch_shapes=scratch,
        compiler_params=pltpu.CompilerParams(
            collective_id=0, has_side_effects=True, vmem_limit_bytes=56 * 1024 * 1024
        ),
        cost_estimate=pl.CostEstimate(flops=4_000_000_000, bytes_accessed=3_000_000, transcendentals=4_000_000),
    )(offsets, queries, key_rows, value_rows, w_out, d_out)


def solution(mesh):
    in_specs = (
        P("seq", "head"),
        P("seq", "head"),
        P("seq", "head"),
        P(None, "head"),
        P("head", None),
        P("seq", "head"),
    )
    out_specs = (P("seq", "head"), P("seq", "head"), P("seq", "head"), P("seq", "head"))
    return jax.shard_map(
        functools.partial(shards, mesh.shape["head"]),
        mesh=mesh,
        in_specs=in_specs,
        out_specs=out_specs,
        check_vma=False,
    )
```

```python
import functools

import jax
import jax.numpy as jnp
from jax import lax
from jax.experimental import pallas as pl
from jax.experimental.pallas import tpu as pltpu
from jax.sharding import PartitionSpec as P

MESH = pl.DeviceIdType.MESH
HD = 64
LEVELS = 4
T = 1024
C = 128
FIRST = (0, 8, 12, 14)
COUNT = (8, 4, 2, 1)
BLOCKS = 15
F32, BF16 = jnp.float32, jnp.bfloat16
W_STEP = 4
D_STEP = 11
PASS_STEP = (0, 0, 7, 9)


def nn(a, b):
    return lax.dot_general(a, b, (((1,), (0,)), ((), ())), preferred_element_type=F32)


def nt(a, b):
    return lax.dot_general(a, b, (((1,), (1,)), ((), ())), preferred_element_type=F32)


def iota(shape, dim):
    return lax.broadcasted_iota(jnp.int32, shape, dim)


def split3(x):
    hi = x.astype(BF16)
    rest = x - hi.astype(F32)
    mid = rest.astype(BF16)
    lo = (rest - mid.astype(F32)).astype(BF16)
    return hi.astype(F32), mid.astype(F32), lo.astype(F32)


def pick_row(row, values):
    out = jnp.zeros_like(values[0] + row.astype(F32))
    for i, value in enumerate(values):
        out = jnp.where(row == i, value, out)
    return out


def kernel(
    nh,
    off,
    q_hbm,
    k_hbm,
    v_hbm,
    w_hbm,
    g_hbm,
    layer_ref,
    dq_ref,
    dk_ref,
    dv_ref,
    q_ref,
    k_ref,
    v_ref,
    w_ref,
    g_ref,
    sel1,
    sel2,
    sel3,
    qt,
    kv1,
    kv2,
    kv3,
    kvt,
    qbd,
    dbd,
    probs,
    grads,
    scores,
    kvs1,
    kvs2,
    kvs3,
    wfull,
    dsend,
    dpass,
    dsum,
    drecv,
    dap,
    toko,
    tokl,
    att,
    dkv,
    dqs,
    gs1,
    gs2,
    gs3,
    gx2,
    gx3,
    gt2,
    gt3,
    gr1,
    gr2,
    gr3,
    own1,
    stk1,
    stk2,
    stk3,
    kv_ss,
    kv_rs,
    gr_ss,
    gr_rs,
    w_ss,
    w_rs,
    d_ss,
    d_rs,
    a_ss,
    a_rs,
    in_sem,
):
    sels = (None, sel1, sel2, sel3)
    kvs = (None, kvs1, kvs2, kvs3)
    kv = (None, kv1, kv2, kv3)
    gsend = (None, gs1, gs2, gs3)
    gother = (None, None, gx2, gx3)
    gtotal = (None, None, gt2, gt3)
    grecv = (None, gr1, gr2, gr3)
    stacks = (None, stk1, stk2, stk3)
    seq = lax.axis_index("seq")
    hx = lax.axis_index("head")
    rank = [lax.rem(seq, 1 << l) for l in range(LEVELS)]
    core = rank[1]
    y = lax.div(rank[3], 2)
    right, left = lax.rem(hx + 1, nh), lax.rem(hx + nh - 1, nh)
    sibling = (seq + 1 - 2 * core, hx)

    def column(l, dy):
        span = 1 << (l - 1)
        at = lax.rem(y, span)
        return y - at + lax.rem(at + dy, span)

    def along(y_to):
        return (seq - rank[3] + y_to * 2 + core, hx)

    def head_peer(d):
        return lax.rem(hx + d, nh)

    def remote(src, dst, sems, i, device):
        return pltpu.make_async_remote_copy(
            src_ref=src,
            dst_ref=dst,
            send_sem=sems[0].at[i],
            recv_sem=sems[1].at[i],
            device_id=device,
            device_id_type=MESH,
        )

    def block(index, size):
        return pl.ds(pl.multiple_of(index * size, size), size)

    def keys(l):
        return k_ref[...] if l == 0 else kv[l][:, 0:128]

    def values(l):
        return v_ref[...] if l == 0 else kv[l][:, 128:256]

    barrier = pltpu.get_barrier_semaphore()
    peers = [sibling] + [along(column(3, dy)) for dy in (1, 2, 3)]
    peers += [(seq, head_peer(d)) for d in range(1, nh)]
    for peer in peers:
        pl.semaphore_signal(barrier, inc=1, device_id=peer, device_id_type=MESH)
    loads = [
        pltpu.make_async_copy(src, dst, in_sem.at[i])
        for i, (src, dst) in enumerate(
            ((w_hbm, w_ref), (k_hbm, k_ref), (v_hbm, v_ref), (q_hbm, q_ref), (g_hbm, g_ref))
        )
    ]
    for load in loads:
        load.start()
    loads[0].wait()
    pl.semaphore_wait(barrier, len(peers))

    own_rows = block(hx, 128)

    def w_copy(d):
        return remote(
            w_ref.at[:, block(head_peer(d), 256)],
            wfull.at[own_rows, :],
            (w_ss, w_rs),
            d - 1,
            (seq, head_peer(d)),
        )

    for d in range(1, nh):
        w_copy(d).start()
    wfull[own_rows, :] = w_ref[:, block(hx, 256)]
    loads[1].wait()
    loads[2].wait()

    lane = iota((1, 256), 1)
    second = lane >= C
    offs = [[lax.rem(off[h, l], 1 << l) for h in range(2)] for l in range(LEVELS)]

    kv_sems = (kv_ss, kv_rs)
    kv_base = (0, 0, 1, 4)

    def kv_own(l):
        return kv[l].at[block(rank[l], T >> l), :]

    def kv_sibling(l):
        return remote(kvs[l], kv_own(l), kv_sems, kv_base[l], sibling)

    def kv_along(l, dy):
        return remote(kvs[l], kv_own(l), kv_sems, kv_base[l] + dy, along(column(l, dy)))

    def kv_pass(l, dy):
        span = 1 << (l - 1)
        source = column(l, span - dy)
        part = kv[l].at[block(lax.rem(source, span) * 2 + core, T >> l), :]
        return remote(part, part, kv_sems, kv_base[l] + span - 1 + dy, sibling)

    kv_head1 = lax.rem(iota((C, 256), 1), 128) >= HD
    for l in (3, 2, 1):
        r = 1 << l
        tok = C * r
        n = T >> l
        row2 = iota((256, tok), 0)
        target = lax.rem(row2, C) * r + jnp.where(row2 >= C, offs[l][1], offs[l][0])
        selt = jnp.where(iota((256, tok), 1) == target, 1.0, 0.0).astype(BF16)
        for c in range(COUNT[l]):
            rows = slice(c * tok, (c + 1) * tok)
            both = nn(selt, jnp.concatenate([k_ref[rows, :], v_ref[rows, :]], axis=1))
            kvs[l][c * C : (c + 1) * C, :] = jnp.where(kv_head1, both[C:], both[:C]).astype(BF16)
        for dy in range(1, r // 2):
            kv_along(l, dy).start()
        kv_sibling(l).start()
        kv[l][block(rank[l], n), :] = kvs[l][...]

    eye = jnp.where(iota((256, 256), 0) == iota((256, 256), 1), 1.0, 0.0).astype(BF16)
    diag = (iota((C, 256), 0) >= HD) == (iota((C, 256), 1) >= C)
    row16 = iota((16, 256), 0)
    own_row = lax.div(row16, 3) == lax.div(iota((16, 256), 1), C)
    top = iota((C, C), 0) < HD
    ones16 = jnp.ones((16, T), BF16)
    ones128 = jnp.ones((T, 128), BF16)
    zeros112 = jnp.zeros((112, 256), BF16)

    loads[3].wait()
    loads[4].wait()
    qt[...] = (nt(eye[:C, :C], q_ref[...]) * 0.125).astype(BF16)

    def place_queries(l):
        tok = C << l
        if l:
            target = lax.rem(lane, C) * (1 << l) + jnp.where(second, offs[l][1], offs[l][0])
            sels[l][...] = jnp.where(iota((tok, 256), 0) == target, 1.0, 0.0).astype(BF16)
        for c in range(COUNT[l]):
            part = qt[:, c * tok : (c + 1) * tok]
            if l == 0:
                both = jnp.concatenate([part, part], axis=1).astype(F32)
            else:
                both = nn(part, sels[l][...])
            qbd[FIRST[l] + c] = jnp.where(diag, both, 0.0).astype(BF16)

    def transpose_kv(l):
        for c in range(4):
            rows = slice(c * 256, (c + 1) * 256)
            if l == 0:
                part = jnp.concatenate([k_ref[rows, :], v_ref[rows, :]], axis=1)
            else:
                part = kv[l][rows, :]
            kvt[l, :, rows] = nt(eye, part).astype(BF16)

    where = [(l, c) for l in range(LEVELS) for c in range(COUNT[l])]
    top_scores = {}

    def score_stage(b):
        l, c = where[b]
        score = nn(keys(l), qbd[b])
        scores[b % 2] = score
        top_scores[b] = jnp.max(score, axis=0, keepdims=True)

    def prob_stage(b):
        probs[b] = jnp.exp(scores[b % 2] - top_scores[b]).astype(BF16)

    def out_stage(b):
        l, c = where[b]
        out = nn(jnp.concatenate([kvt[l, 128:256, :], ones16], axis=0), probs[b])
        total = out[C : C + 1]
        lse = top_scores[b] + jnp.log(total)
        out = out[:C] * (1.0 / total)
        if l == 0:
            cols = slice(c * C, (c + 1) * C)
            toko[0, :, cols] = jnp.where(top, out[:, :C], out[:, C:])
            tokl[0, 0:1, cols] = lse[:, :C]
            tokl[0, 1:2, cols] = lse[:, C:]
            return
        r = 1 << l
        tok = C * r
        cols = slice(c * tok, (c + 1) * tok)
        pieces = pick_row(lax.rem(row16, 3), split3(lse))
        pieces = jnp.where(own_row, pieces, 0.0)
        packed = jnp.concatenate([jnp.where(diag, out, 0.0), pieces], axis=0).astype(BF16)
        placed = nt(packed, sels[l][...])
        toko[l, :, cols] = placed[:C]
        phase = lax.rem(iota((1, tok), 1), r)
        for h in range(2):
            i = C + 3 * h
            value = placed[i : i + 1] + placed[i + 1 : i + 2] + placed[i + 2 : i + 3]
            tokl[l, h : h + 1, cols] = jnp.where(phase == offs[l][h], value, -1e30)

    d_sems = (d_ss, d_rs)
    halves = (pl.ds(0, 512), pl.ds(512, 512))
    sides = (right, left)
    rows_of = [block(x, 128) for x in sides]
    opposite = head_peer(2)

    def d_over(i):
        return remote(
            dsend.at[block(opposite, 128), halves[i]],
            dpass.at[i],
            d_sems,
            i,
            (seq, sides[i]),
        )

    def d_plain(i):
        return remote(
            dsend.at[rows_of[i], halves[1 - i]],
            drecv.at[i, :, halves[1 - i]],
            d_sems,
            2 + i,
            (seq, sides[i]),
        )

    def d_summed(i):
        return remote(dsum.at[i], drecv.at[i, :, halves[i]], d_sems, 4 + i, (seq, sides[i]))

    place_queries(0)
    for step in range(BLOCKS + 2):
        if step == W_STEP:
            for d in range(1, nh):
                w_copy(d).wait_recv()
            for c in range(4):
                cols = slice(c * 256, (c + 1) * 256)
                dsend[:, cols] = nt(wfull[...], g_ref[cols, :]).astype(BF16)
            for i in range(2):
                d_over(i).start()
            for i in range(2):
                d_plain(i).start()
        if step == D_STEP:
            for i in range(2):
                d_over(i).wait_recv()
            for i in range(2):
                dsum[i] = (
                    dsend[rows_of[i], halves[i]].astype(F32) + dpass[i].astype(F32)
                ).astype(BF16)
                d_summed(i).start()
        for l in (2, 3):
            if step == PASS_STEP[l]:
                for dy in range(1, 1 << (l - 1)):
                    kv_along(l, dy).wait_recv()
                    kv_pass(l, dy).start()
        if step in FIRST[1:]:
            l = FIRST.index(step)
            kv_sibling(l).wait_recv()
            for dy in range(1, 1 << (l - 1)):
                kv_pass(l, dy).wait_recv()
            transpose_kv(l)
        if step < BLOCKS:
            score_stage(step)
        if step == 0:
            transpose_kv(0)
        if step in (1, 2, 3):
            place_queries(step)
        if 0 <= step - 1 < BLOCKS:
            prob_stage(step - 1)
        if 0 <= step - 2:
            out_stage(step - 2)

    lses = [tokl[l, 0:2, :] for l in range(LEVELS)]
    peak = jnp.maximum(jnp.maximum(lses[0], lses[1]), jnp.maximum(lses[2], lses[3]))
    total = sum(jnp.exp(x - peak) for x in lses)
    joint = peak + jnp.log(total)
    is_top = iota((C, T), 0) < HD
    mixed = jnp.zeros((C, T), F32)
    for l in range(LEVELS):
        weight = jnp.exp(lses[l] - joint)
        mixed = mixed + jnp.where(is_top, weight[0:1], weight[1:2]) * toko[l]
    mixed_b = mixed.astype(BF16)
    dap[128:256, :] = mixed_b
    att[:, own_rows] = mixed_b.astype(F32).T.astype(BF16)

    a_sems = (a_ss, a_rs)

    def a_own(i, half):
        part = att.at[halves[half], own_rows]
        return remote(part, part, a_sems, i + (0 if half == i else 2), (seq, sides[i]))

    def a_pass(i):
        part = att.at[halves[i], rows_of[1 - i]]
        return remote(part, part, a_sems, 4 + i, (seq, sides[i]))

    for i in range(2):
        a_own(i, i).start()
    for i in range(2):
        a_own(i, 1 - i).start()

    rowt = iota((16, T), 0)
    hi, mid, lo = split3(joint)
    dap[256:272, :] = pick_row(
        rowt, (hi[0:1], mid[0:1], lo[0:1], hi[1:2], mid[1:2], lo[1:2])
    ).astype(BF16)

    for i in range(2):
        d_plain(i).wait_recv()
    for i in range(2):
        d_summed(i).wait_recv()
    d_sum = dsend[own_rows, :].astype(F32) + drecv[0].astype(F32) + drecv[1].astype(F32)
    dap[0:128, :] = d_sum.astype(BF16)

    def prepare(b):
        l, c = where[b]
        tok = C << l
        part = dap[:, c * tok : (c + 1) * tok]
        if l == 0:
            both = jnp.concatenate([part, part], axis=1).astype(F32)
        else:
            both = nn(part, sels[l][...])
        x = both[256:272]
        lse = jnp.where(second, x[3:4] + x[4:5] + x[5:6], x[0:1] + x[1:2] + x[2:3])
        coef = jnp.exp(top_scores[b] - lse)
        d_b = jnp.where(diag, both[0:128] * coef, 0.0).astype(BF16)
        dbd[b, 0:128, :] = d_b
        delta = jnp.sum(d_b.astype(F32) * both[128:256], axis=0, keepdims=True)
        dbd[b, 128:144, :] = pick_row(row16, [-x for x in split3(delta)]).astype(BF16)

    def grad_stage(b):
        l, c = where[b]
        d_prob = nn(
            jnp.concatenate([values(l), ones128], axis=1),
            jnp.concatenate([dbd[b], zeros112], axis=0),
        )
        grads[b] = probs[b] * d_prob.astype(BF16)

    def query_stage(b):
        l, c = where[b]
        d_q = nn(kvt[l, 0:128, :], grads[b]) * 0.125
        if l == 0:
            dqs[b] = jnp.where(top, d_q[:, :C], d_q[:, C:]).T
        else:
            qbd[b] = jnp.where(diag, d_q, 0.0).astype(BF16)

    def side(refs):
        return jnp.concatenate(refs, axis=1)

    def key_stage(blocks, fresh):
        d_k = nt(side([grads[b] for b in blocks]), side([qbd[b] for b in blocks]))
        d_v = nt(side([probs[b] for b in blocks]), side([dbd[b, 0:128, :] for b in blocks]))
        if fresh:
            dkv[:, 0:128] = d_k
            dkv[:, 128:256] = d_v
        else:
            dkv[:, 0:128] += d_k
            dkv[:, 128:256] += d_v

    g_sems = (gr_ss, gr_rs)
    g_base = (0, 0, 1, 3)

    def g_sibling(l):
        to = gr1.at[0] if l == 1 else gother[l]
        part = gsend[l].at[1 - core, 0] if l == 1 else gsend[l].at[1 - core]
        return remote(part, to, g_sems, g_base[l], sibling)

    def g_along(l, dy):
        to = column(l, dy)
        part = gtotal[l].at[lax.rem(to, 1 << (l - 1))]
        return remote(part, grecv[l].at[dy - 1], g_sems, g_base[l] + dy, along(to))

    def send_sibling(l):
        n = T >> l
        for i in range(1 << l):
            gsend[l][i % 2, i // 2] = dkv[i * n : (i + 1) * n, :].astype(BF16)
        g_sibling(l).start()
        if l == 1:
            own1[...] = dkv[block(rank[1], n), :]

    def send_along(l):
        g_sibling(l).wait_recv()
        gtotal[l][...] = (gsend[l][core].astype(F32) + gother[l][...].astype(F32)).astype(BF16)
        for dy in range(1, 1 << (l - 1)):
            g_along(l, dy).start()

    def stack_level(l):
        for c in range(COUNT[l]):
            rows = slice(c * C, (c + 1) * C)
            if l == 1:
                grad = own1[rows, :] + gr1[0, rows, :].astype(F32)
            else:
                grad = gtotal[l][lax.rem(y, 1 << (l - 1)), rows, :].astype(F32)
                for dy in range(1, 1 << (l - 1)):
                    grad = grad + grecv[l][dy - 1, rows, :].astype(F32)
            stacks[l][c, 0:C, :] = jnp.where(kv_head1, 0.0, grad).astype(BF16)
            stacks[l][c, C:256, :] = jnp.where(kv_head1, grad, 0.0).astype(BF16)

    def finish_group(group):
        key_stage(group, group[0] != 4)
        for b in group:
            query_stage(b)

    def grad_group(group):
        for b in group:
            prepare(b)
            grad_stage(b)

    groups = [[14], [12, 13], [8, 9, 10, 11], [0, 1, 2, 3], [4, 5, 6, 7]]
    grad_group(groups[0])
    grad_group(groups[1])
    finish_group(groups[0])
    send_sibling(3)
    grad_group(groups[2])
    finish_group(groups[1])
    send_sibling(2)
    send_along(3)
    grad_group(groups[3])
    finish_group(groups[2])
    send_sibling(1)
    send_along(2)
    for i in range(2):
        a_own(i, i).wait_recv()
        a_pass(i).start()
    grad_group(groups[4])
    finish_group(groups[3])
    for i in range(2):
        a_own(i, 1 - i).wait_recv()
    for i in range(2):
        a_pass(i).wait_recv()
    for l in (3, 2):
        for dy in range(1, 1 << (l - 1)):
            g_along(l, dy).wait_recv()
    g_sibling(1).wait_recv()
    finish_group(groups[4])

    layer_ref[...] = nn(att[...], wfull[...]).astype(BF16)

    for l in (3, 2, 1):
        stack_level(l)
    for c in range(4):
        rows = slice(c * 256, (c + 1) * 256)
        place = side([sel1[...], sel2[c % 2 * 256 : c % 2 * 256 + 256, :], sel3[rows, :]])
        d_q = nt(place, side([qbd[8 + c], qbd[12 + c // 2], qbd[14]]))
        for half in range(2):
            part = slice(half * C, half * C + C)
            d_rows = slice(c * 256 + half * C, c * 256 + half * C + C)
            dq_ref[d_rows, :] = (d_q[part] + dqs[2 * c + half]).astype(BF16)
        d_kv = dkv[rows, :] + nn(
            place, jnp.concatenate([stk1[c], stk2[c // 2], stk3[0]], axis=0)
        )
        dk_ref[rows, :] = d_kv[:, 0:128].astype(BF16)
        dv_ref[rows, :] = d_kv[:, 128:256].astype(BF16)

    for d in range(1, nh):
        w_copy(d).wait_send()
    for i in range(2):
        for copy in (d_over(i), d_plain(i), d_summed(i), a_own(i, 0), a_own(i, 1), a_pass(i)):
            copy.wait_send()
    for l in (1, 2, 3):
        kv_sibling(l).wait_send()
        g_sibling(l).wait_send()
        for dy in range(1, 1 << (l - 1)):
            kv_along(l, dy).wait_send()
            kv_pass(l, dy).wait_send()
            g_along(l, dy).wait_send()


def hand_out(*refs):
    sems = refs[8]
    copies = [pltpu.make_async_copy(refs[i], refs[4 + i], sems.at[i]) for i in range(4)]
    for copy in copies:
        copy.start()
    for copy in copies:
        copy.wait()


def shards(nh, queries, key_rows, value_rows, offsets, w_out, d_out):
    vmem = pl.BlockSpec(memory_space=pltpu.VMEM)
    dma = pltpu.SemaphoreType.DMA
    feat = 128 * nh
    scratch = [
        *[pltpu.VMEM((T, 128), BF16)] * 3,
        pltpu.VMEM((128, feat * 2), BF16),
        pltpu.VMEM((T, 256), BF16),
        *[pltpu.VMEM((C << l, 256), BF16) for l in (1, 2, 3)],
        pltpu.VMEM((128, T), BF16),
        *[pltpu.VMEM((T, 256), BF16) for l in (1, 2, 3)],
        pltpu.VMEM((LEVELS, 256, T), BF16),
        pltpu.VMEM((BLOCKS, 128, 256), BF16),
        pltpu.VMEM((BLOCKS, 144, 256), BF16),
        pltpu.VMEM((BLOCKS, T, 256), BF16),
        pltpu.VMEM((BLOCKS, T, 256), BF16),
        pltpu.VMEM((2, T, 256), F32),
        *[pltpu.VMEM((T >> l, 256), BF16) for l in (1, 2, 3)],
        pltpu.VMEM((feat, 256), BF16),
        pltpu.VMEM((feat, T), BF16),
        pltpu.VMEM((2, 128, 512), BF16),
        pltpu.VMEM((2, 128, 512), BF16),
        pltpu.VMEM((2, 128, T), BF16),
        pltpu.VMEM((272, T), BF16),
        pltpu.VMEM((LEVELS, 128, T), F32),
        pltpu.VMEM((LEVELS, 8, T), F32),
        pltpu.VMEM((T, feat), BF16),
        pltpu.VMEM((T, 256), F32),
        pltpu.VMEM((8, C, 128), F32),
        *[pltpu.VMEM((2, (1 << l) // 2, T >> l, 256), BF16) for l in (1, 2, 3)],
        *[pltpu.VMEM(((1 << l) // 2, T >> l, 256), BF16) for l in (2, 3)],
        *[pltpu.VMEM(((1 << l) // 2, T >> l, 256), BF16) for l in (2, 3)],
        *[pltpu.VMEM((max((1 << l) // 2 - 1, 1), T >> l, 256), BF16) for l in (1, 2, 3)],
        pltpu.VMEM((T // 2, 256), F32),
        *[pltpu.VMEM((COUNT[l], 256, 256), BF16) for l in (1, 2, 3)],
        dma((11,)),
        dma((11,)),
        dma((7,)),
        dma((7,)),
        dma((nh - 1,)),
        dma((nh - 1,)),
        *[dma((6,))] * 4,
        dma((5,)),
    ]
    outs = pl.pallas_call(
        functools.partial(kernel, nh),
        out_shape=(
            pltpu.VMEM((T, 256), BF16),
            pltpu.VMEM((T, 128), BF16),
            pltpu.VMEM((T, 128), BF16),
            pltpu.VMEM((T, 128), BF16),
        ),
        in_specs=[pl.BlockSpec(memory_space=pltpu.SMEM)] + [pl.BlockSpec(memory_space=pl.ANY)] * 5,
        out_specs=(vmem,) * 4,
        scratch_shapes=scratch,
        compiler_params=pltpu.CompilerParams(
            collective_id=0, has_side_effects=True, vmem_limit_bytes=56 * 1024 * 1024
        ),
        cost_estimate=pl.CostEstimate(flops=4_000_000_000, bytes_accessed=3_000_000, transcendentals=4_000_000),
    )(offsets.T, queries, key_rows, value_rows, w_out, d_out)

    anyspec = pl.BlockSpec(memory_space=pl.ANY)
    outs = [pltpu.with_memory_space_constraint(x, pltpu.VMEM) for x in outs]
    return pl.pallas_call(
        hand_out,
        out_shape=tuple(jax.ShapeDtypeStruct(x.shape, x.dtype) for x in outs),
        in_specs=[vmem] * 4,
        out_specs=(anyspec,) * 4,
        scratch_shapes=[dma((4,))],
    )(*outs)


def solution(mesh):
    in_specs = (
        P("seq", "head"),
        P("seq", "head"),
        P("seq", "head"),
        P(None, "head"),
        P("head", None),
        P("seq", "head"),
    )
    out_specs = (P("seq", "head"), P("seq", "head"), P("seq", "head"), P("seq", "head"))
    return jax.shard_map(
        functools.partial(shards, mesh.shape["head"]),
        mesh=mesh,
        in_specs=in_specs,
        out_specs=out_specs,
        check_vma=False,
    )
```

```python
import functools

import jax
import jax.numpy as jnp
from jax import lax
from jax.experimental import pallas as pl
from jax.experimental.pallas import tpu as pltpu
from jax.sharding import PartitionSpec as P

MESH = pl.DeviceIdType.MESH
HD = 64
LEVELS = 4
T = 1024
C = 128
FIRST = (0, 8, 12, 14)
COUNT = (8, 4, 2, 1)
BLOCKS = 15
F32, BF16 = jnp.float32, jnp.bfloat16
W_STEP = 3
D_STEP = 11
PASS_STEP = (0, 0, 10, 12)


def nn(a, b):
    return lax.dot_general(a, b, (((1,), (0,)), ((), ())), preferred_element_type=F32)


def nt(a, b):
    return lax.dot_general(a, b, (((1,), (1,)), ((), ())), preferred_element_type=F32)


def iota(shape, dim):
    return lax.broadcasted_iota(jnp.int32, shape, dim)


def split3(x):
    hi = x.astype(BF16)
    rest = x - hi.astype(F32)
    mid = rest.astype(BF16)
    lo = (rest - mid.astype(F32)).astype(BF16)
    return hi.astype(F32), mid.astype(F32), lo.astype(F32)


def pick_row(row, values):
    out = jnp.zeros_like(values[0] + row.astype(F32))
    for i, value in enumerate(values):
        out = jnp.where(row == i, value, out)
    return out


def kernel(
    nh,
    off,
    q_hbm,
    k_hbm,
    v_hbm,
    w_hbm,
    g_hbm,
    layer_ref,
    dq_ref,
    dk_ref,
    dv_ref,
    q_ref,
    k_ref,
    v_ref,
    w_ref,
    g_ref,
    sel1,
    sel2,
    sel3,
    qt,
    kv1,
    kv2,
    kv3,
    kvt,
    qbd,
    dbd,
    probs,
    grads,
    scores,
    kvs1,
    kvs2,
    kvs3,
    wfull,
    dsend,
    dpass,
    dsum,
    drecv,
    dap,
    toko,
    tokl,
    att,
    dkv,
    dqs,
    gs1,
    gs2,
    gs3,
    gx2,
    gx3,
    gt2,
    gt3,
    gr1,
    gr2,
    gr3,
    own1,
    stk1,
    stk2,
    stk3,
    kv_ss,
    kv_rs,
    gr_ss,
    gr_rs,
    w_ss,
    w_rs,
    d_ss,
    d_rs,
    a_ss,
    a_rs,
    in_sem,
):
    sels = (None, sel1, sel2, sel3)
    kvs = (None, kvs1, kvs2, kvs3)
    kv = (None, kv1, kv2, kv3)
    gsend = (None, gs1, gs2, gs3)
    gother = (None, None, gx2, gx3)
    gtotal = (None, None, gt2, gt3)
    grecv = (None, gr1, gr2, gr3)
    stacks = (None, stk1, stk2, stk3)
    seq = lax.axis_index("seq")
    hx = lax.axis_index("head")
    rank = [lax.rem(seq, 1 << l) for l in range(LEVELS)]
    core = rank[1]
    y = lax.div(rank[3], 2)
    right, left = lax.rem(hx + 1, nh), lax.rem(hx + nh - 1, nh)
    sibling = (seq + 1 - 2 * core, hx)

    def column(l, dy):
        span = 1 << (l - 1)
        at = lax.rem(y, span)
        return y - at + lax.rem(at + dy, span)

    def along(y_to):
        return (seq - rank[3] + y_to * 2 + core, hx)

    def head_peer(d):
        return lax.rem(hx + d, nh)

    def remote(src, dst, sems, i, device):
        return pltpu.make_async_remote_copy(
            src_ref=src,
            dst_ref=dst,
            send_sem=sems[0].at[i],
            recv_sem=sems[1].at[i],
            device_id=device,
            device_id_type=MESH,
        )

    def block(index, size):
        return pl.ds(pl.multiple_of(index * size, size), size)

    def keys(l):
        return k_ref[...] if l == 0 else kv[l][:, 0:128]

    def values(l):
        return v_ref[...] if l == 0 else kv[l][:, 128:256]

    barrier = pltpu.get_barrier_semaphore()
    peers = [sibling] + [along(column(3, dy)) for dy in (1, 2, 3)]
    peers += [(seq, head_peer(d)) for d in range(1, nh)]
    for peer in peers:
        pl.semaphore_signal(barrier, inc=1, device_id=peer, device_id_type=MESH)
    loads = [
        pltpu.make_async_copy(src, dst, in_sem.at[i])
        for i, (src, dst) in enumerate(
            ((w_hbm, w_ref), (k_hbm, k_ref), (v_hbm, v_ref), (q_hbm, q_ref), (g_hbm, g_ref))
        )
    ]
    for load in loads:
        load.start()
    loads[0].wait()
    pl.semaphore_wait(barrier, len(peers))

    own_rows = block(hx, 128)

    def w_copy(d):
        return remote(
            w_ref.at[:, block(head_peer(d), 256)],
            wfull.at[own_rows, :],
            (w_ss, w_rs),
            d - 1,
            (seq, head_peer(d)),
        )

    for d in range(1, nh):
        w_copy(d).start()
    wfull[own_rows, :] = w_ref[:, block(hx, 256)]
    loads[1].wait()
    loads[2].wait()

    lane = iota((1, 256), 1)
    second = lane >= C
    offs = [[lax.rem(off[h, l], 1 << l) for h in range(2)] for l in range(LEVELS)]

    kv_sems = (kv_ss, kv_rs)
    kv_base = (0, 0, 1, 4)

    def kv_own(l):
        return kv[l].at[block(rank[l], T >> l), :]

    def kv_sibling(l):
        return remote(kvs[l], kv_own(l), kv_sems, kv_base[l], sibling)

    def kv_along(l, dy):
        return remote(kvs[l], kv_own(l), kv_sems, kv_base[l] + dy, along(column(l, dy)))

    def kv_pass(l, dy):
        span = 1 << (l - 1)
        source = column(l, span - dy)
        part = kv[l].at[block(lax.rem(source, span) * 2 + core, T >> l), :]
        return remote(part, part, kv_sems, kv_base[l] + span - 1 + dy, sibling)

    kv_head1 = lax.rem(iota((C, 256), 1), 128) >= HD
    for l in (3, 2, 1):
        r = 1 << l
        tok = C * r
        n = T >> l
        row2 = iota((256, tok), 0)
        target = lax.rem(row2, C) * r + jnp.where(row2 >= C, offs[l][1], offs[l][0])
        selt = jnp.where(iota((256, tok), 1) == target, 1.0, 0.0).astype(BF16)
        for c in range(COUNT[l]):
            rows = slice(c * tok, (c + 1) * tok)
            both = nn(selt, jnp.concatenate([k_ref[rows, :], v_ref[rows, :]], axis=1))
            kvs[l][c * C : (c + 1) * C, :] = jnp.where(kv_head1, both[C:], both[:C]).astype(BF16)
        for dy in range(1, r // 2):
            kv_along(l, dy).start()
        kv_sibling(l).start()
        kv[l][block(rank[l], n), :] = kvs[l][...]

    eye = jnp.where(iota((256, 256), 0) == iota((256, 256), 1), 1.0, 0.0).astype(BF16)
    diag = (iota((C, 256), 0) >= HD) == (iota((C, 256), 1) >= C)
    row16 = iota((16, 256), 0)
    own_row = lax.div(row16, 3) == lax.div(iota((16, 256), 1), C)
    top = iota((C, C), 0) < HD
    ones16 = jnp.ones((16, T), BF16)
    ones128 = jnp.ones((T, 128), BF16)
    zeros112 = jnp.zeros((112, 256), BF16)

    loads[3].wait()
    loads[4].wait()
    qt[...] = (nt(eye[:C, :C], q_ref[...]) * 0.125).astype(BF16)

    def place_queries(l):
        tok = C << l
        if l:
            target = lax.rem(lane, C) * (1 << l) + jnp.where(second, offs[l][1], offs[l][0])
            sels[l][...] = jnp.where(iota((tok, 256), 0) == target, 1.0, 0.0).astype(BF16)
        for c in range(COUNT[l]):
            part = qt[:, c * tok : (c + 1) * tok]
            if l == 0:
                both = jnp.concatenate([part, part], axis=1).astype(F32)
            else:
                both = nn(part, sels[l][...])
            qbd[FIRST[l] + c] = jnp.where(diag, both, 0.0).astype(BF16)

    def transpose_kv(l):
        for c in range(4):
            rows = slice(c * 256, (c + 1) * 256)
            if l == 0:
                part = jnp.concatenate([k_ref[rows, :], v_ref[rows, :]], axis=1)
            else:
                part = kv[l][rows, :]
            kvt[l, :, rows] = nt(eye, part).astype(BF16)

    where = [(l, c) for l in range(LEVELS) for c in range(COUNT[l])]
    top_scores = {}

    def score_stage(b):
        l, c = where[b]
        score = nn(keys(l), qbd[b])
        scores[b % 2] = score
        top_scores[b] = jnp.max(score, axis=0, keepdims=True)

    def prob_stage(b):
        probs[b] = jnp.exp(scores[b % 2] - top_scores[b]).astype(BF16)

    def out_stage(b):
        l, c = where[b]
        out = nn(jnp.concatenate([kvt[l, 128:256, :], ones16], axis=0), probs[b])
        total = out[C : C + 1]
        lse = top_scores[b] + jnp.log(total)
        out = out[:C] * (1.0 / total)
        if l == 0:
            cols = slice(c * C, (c + 1) * C)
            toko[0, :, cols] = jnp.where(top, out[:, :C], out[:, C:])
            tokl[0, 0:1, cols] = lse[:, :C]
            tokl[0, 1:2, cols] = lse[:, C:]
            return
        r = 1 << l
        tok = C * r
        cols = slice(c * tok, (c + 1) * tok)
        pieces = pick_row(lax.rem(row16, 3), split3(lse))
        pieces = jnp.where(own_row, pieces, 0.0)
        packed = jnp.concatenate([jnp.where(diag, out, 0.0), pieces], axis=0).astype(BF16)
        placed = nt(packed, sels[l][...])
        toko[l, :, cols] = placed[:C]
        phase = lax.rem(iota((1, tok), 1), r)
        for h in range(2):
            i = C + 3 * h
            value = placed[i : i + 1] + placed[i + 1 : i + 2] + placed[i + 2 : i + 3]
            tokl[l, h : h + 1, cols] = jnp.where(phase == offs[l][h], value, -1e30)

    d_sems = (d_ss, d_rs)
    halves = (pl.ds(0, 512), pl.ds(512, 512))
    sides = (right, left)
    rows_of = [block(x, 128) for x in sides]
    opposite = head_peer(2)

    def d_over(i):
        return remote(
            dsend.at[block(opposite, 128), halves[i]],
            dpass.at[i],
            d_sems,
            i,
            (seq, sides[i]),
        )

    def d_plain(i):
        return remote(
            dsend.at[rows_of[i], halves[1 - i]],
            drecv.at[i, :, halves[1 - i]],
            d_sems,
            2 + i,
            (seq, sides[i]),
        )

    def d_summed(i):
        return remote(dsum.at[i], drecv.at[i, :, halves[i]], d_sems, 4 + i, (seq, sides[i]))

    place_queries(0)
    for step in range(BLOCKS + 2):
        if step == W_STEP:
            for d in range(1, nh):
                w_copy(d).wait_recv()
            for c in range(4):
                cols = slice(c * 256, (c + 1) * 256)
                dsend[:, cols] = nt(wfull[...], g_ref[cols, :]).astype(BF16)
            for i in range(2):
                d_over(i).start()
            for i in range(2):
                d_plain(i).start()
        if step == D_STEP:
            for i in range(2):
                d_over(i).wait_recv()
            for i in range(2):
                dsum[i] = (
                    dsend[rows_of[i], halves[i]].astype(F32) + dpass[i].astype(F32)
                ).astype(BF16)
                d_summed(i).start()
        for l in (2, 3):
            if step == PASS_STEP[l]:
                for dy in range(1, 1 << (l - 1)):
                    kv_along(l, dy).wait_recv()
                    kv_pass(l, dy).start()
        if step in FIRST[1:]:
            l = FIRST.index(step)
            kv_sibling(l).wait_recv()
            for dy in range(1, 1 << (l - 1)):
                kv_pass(l, dy).wait_recv()
            transpose_kv(l)
        if step < BLOCKS:
            score_stage(step)
        if step == 0:
            transpose_kv(0)
        if step in (1, 2, 3):
            place_queries(step)
        if 0 <= step - 1 < BLOCKS:
            prob_stage(step - 1)
        if 0 <= step - 2:
            out_stage(step - 2)

    lses = [tokl[l, 0:2, :] for l in range(LEVELS)]
    peak = jnp.maximum(jnp.maximum(lses[0], lses[1]), jnp.maximum(lses[2], lses[3]))
    total = sum(jnp.exp(x - peak) for x in lses)
    joint = peak + jnp.log(total)
    is_top = iota((C, T), 0) < HD
    mixed = jnp.zeros((C, T), F32)
    for l in range(LEVELS):
        weight = jnp.exp(lses[l] - joint)
        mixed = mixed + jnp.where(is_top, weight[0:1], weight[1:2]) * toko[l]
    mixed_b = mixed.astype(BF16)
    dap[128:256, :] = mixed_b
    att[:, own_rows] = mixed_b.astype(F32).T.astype(BF16)

    a_sems = (a_ss, a_rs)

    def a_own(i, half):
        part = att.at[halves[half], own_rows]
        return remote(part, part, a_sems, i + (0 if half == i else 2), (seq, sides[i]))

    def a_pass(i):
        part = att.at[halves[i], rows_of[1 - i]]
        return remote(part, part, a_sems, 4 + i, (seq, sides[i]))

    for i in range(2):
        a_own(i, i).start()
    for i in range(2):
        a_own(i, 1 - i).start()

    rowt = iota((16, T), 0)
    hi, mid, lo = split3(joint)
    dap[256:272, :] = pick_row(
        rowt, (hi[0:1], mid[0:1], lo[0:1], hi[1:2], mid[1:2], lo[1:2])
    ).astype(BF16)

    for i in range(2):
        d_plain(i).wait_recv()
    for i in range(2):
        d_summed(i).wait_recv()
    d_sum = dsend[own_rows, :].astype(F32) + drecv[0].astype(F32) + drecv[1].astype(F32)
    dap[0:128, :] = d_sum.astype(BF16)

    def prepare(b):
        l, c = where[b]
        tok = C << l
        part = dap[:, c * tok : (c + 1) * tok]
        if l == 0:
            both = jnp.concatenate([part, part], axis=1).astype(F32)
        else:
            both = nn(part, sels[l][...])
        x = both[256:272]
        lse = jnp.where(second, x[3:4] + x[4:5] + x[5:6], x[0:1] + x[1:2] + x[2:3])
        coef = jnp.exp(top_scores[b] - lse)
        d_b = jnp.where(diag, both[0:128] * coef, 0.0).astype(BF16)
        dbd[b, 0:128, :] = d_b
        delta = jnp.sum(d_b.astype(F32) * both[128:256], axis=0, keepdims=True)
        dbd[b, 128:144, :] = pick_row(row16, [-x for x in split3(delta)]).astype(BF16)

    def grad_stage(b):
        l, c = where[b]
        d_prob = nn(
            jnp.concatenate([values(l), ones128], axis=1),
            jnp.concatenate([dbd[b], zeros112], axis=0),
        )
        grads[b] = probs[b] * d_prob.astype(BF16)

    def query_stage(b):
        l, c = where[b]
        d_q = nn(kvt[l, 0:128, :], grads[b]) * 0.125
        if l == 0:
            dqs[b] = jnp.where(top, d_q[:, :C], d_q[:, C:]).T
        else:
            qbd[b] = jnp.where(diag, d_q, 0.0).astype(BF16)

    def side(refs):
        return jnp.concatenate(refs, axis=1)

    def key_stage(blocks, fresh):
        d_k = nt(side([grads[b] for b in blocks]), side([qbd[b] for b in blocks]))
        d_v = nt(side([probs[b] for b in blocks]), side([dbd[b, 0:128, :] for b in blocks]))
        if fresh:
            dkv[:, 0:128] = d_k
            dkv[:, 128:256] = d_v
        else:
            dkv[:, 0:128] += d_k
            dkv[:, 128:256] += d_v

    g_sems = (gr_ss, gr_rs)
    g_base = (0, 0, 1, 3)

    def g_sibling(l):
        to = gr1.at[0] if l == 1 else gother[l]
        part = gsend[l].at[1 - core, 0] if l == 1 else gsend[l].at[1 - core]
        return remote(part, to, g_sems, g_base[l], sibling)

    def g_along(l, dy):
        to = column(l, dy)
        part = gtotal[l].at[lax.rem(to, 1 << (l - 1))]
        return remote(part, grecv[l].at[dy - 1], g_sems, g_base[l] + dy, along(to))

    def send_sibling(l):
        n = T >> l
        for i in range(1 << l):
            gsend[l][i % 2, i // 2] = dkv[i * n : (i + 1) * n, :].astype(BF16)
        g_sibling(l).start()
        if l == 1:
            own1[...] = dkv[block(rank[1], n), :]

    def send_along(l):
        g_sibling(l).wait_recv()
        gtotal[l][...] = (gsend[l][core].astype(F32) + gother[l][...].astype(F32)).astype(BF16)
        for dy in range(1, 1 << (l - 1)):
            g_along(l, dy).start()

    def stack_level(l):
        for c in range(COUNT[l]):
            rows = slice(c * C, (c + 1) * C)
            if l == 1:
                grad = own1[rows, :] + gr1[0, rows, :].astype(F32)
            else:
                grad = gtotal[l][lax.rem(y, 1 << (l - 1)), rows, :].astype(F32)
                for dy in range(1, 1 << (l - 1)):
                    grad = grad + grecv[l][dy - 1, rows, :].astype(F32)
            stacks[l][c, 0:C, :] = jnp.where(kv_head1, 0.0, grad).astype(BF16)
            stacks[l][c, C:256, :] = jnp.where(kv_head1, grad, 0.0).astype(BF16)

    def finish_group(group):
        key_stage(group, group[0] != 4)
        for b in group:
            query_stage(b)

    def grad_group(group):
        for b in group:
            prepare(b)
            grad_stage(b)

    groups = [[14], [12, 13], [8, 9, 10, 11], [0, 1, 2, 3], [4, 5, 6, 7]]
    grad_group(groups[0])
    grad_group(groups[1])
    finish_group(groups[0])
    send_sibling(3)
    grad_group(groups[2])
    finish_group(groups[1])
    send_sibling(2)
    send_along(3)
    grad_group(groups[3])
    finish_group(groups[2])
    send_sibling(1)
    send_along(2)
    for i in range(2):
        a_own(i, i).wait_recv()
        a_pass(i).start()
    grad_group(groups[4])
    finish_group(groups[3])
    for i in range(2):
        a_own(i, 1 - i).wait_recv()
    for i in range(2):
        a_pass(i).wait_recv()
    for l in (3, 2):
        for dy in range(1, 1 << (l - 1)):
            g_along(l, dy).wait_recv()
    g_sibling(1).wait_recv()
    finish_group(groups[4])

    layer_ref[...] = nn(att[...], wfull[...]).astype(BF16)

    for l in (3, 2, 1):
        stack_level(l)
    for c in range(4):
        rows = slice(c * 256, (c + 1) * 256)
        place = side([sel1[...], sel2[c % 2 * 256 : c % 2 * 256 + 256, :], sel3[rows, :]])
        d_q = nt(place, side([qbd[8 + c], qbd[12 + c // 2], qbd[14]]))
        for half in range(2):
            part = slice(half * C, half * C + C)
            d_rows = slice(c * 256 + half * C, c * 256 + half * C + C)
            dq_ref[d_rows, :] = (d_q[part] + dqs[2 * c + half]).astype(BF16)
        d_kv = dkv[rows, :] + nn(
            place, jnp.concatenate([stk1[c], stk2[c // 2], stk3[0]], axis=0)
        )
        dk_ref[rows, :] = d_kv[:, 0:128].astype(BF16)
        dv_ref[rows, :] = d_kv[:, 128:256].astype(BF16)

    for d in range(1, nh):
        w_copy(d).wait_send()
    for i in range(2):
        for copy in (d_over(i), d_plain(i), d_summed(i), a_own(i, 0), a_own(i, 1), a_pass(i)):
            copy.wait_send()
    for l in (1, 2, 3):
        kv_sibling(l).wait_send()
        g_sibling(l).wait_send()
        for dy in range(1, 1 << (l - 1)):
            kv_along(l, dy).wait_send()
            kv_pass(l, dy).wait_send()
            g_along(l, dy).wait_send()


def hand_out(*refs):
    sems = refs[8]
    copies = [pltpu.make_async_copy(refs[i], refs[4 + i], sems.at[i]) for i in range(4)]
    for copy in copies:
        copy.start()
    for copy in copies:
        copy.wait()


def shards(nh, queries, key_rows, value_rows, offsets, w_out, d_out):
    vmem = pl.BlockSpec(memory_space=pltpu.VMEM)
    dma = pltpu.SemaphoreType.DMA
    feat = 128 * nh
    scratch = [
        *[pltpu.VMEM((T, 128), BF16)] * 3,
        pltpu.VMEM((128, feat * 2), BF16),
        pltpu.VMEM((T, 256), BF16),
        *[pltpu.VMEM((C << l, 256), BF16) for l in (1, 2, 3)],
        pltpu.VMEM((128, T), BF16),
        *[pltpu.VMEM((T, 256), BF16) for l in (1, 2, 3)],
        pltpu.VMEM((LEVELS, 256, T), BF16),
        pltpu.VMEM((BLOCKS, 128, 256), BF16),
        pltpu.VMEM((BLOCKS, 144, 256), BF16),
        pltpu.VMEM((BLOCKS, T, 256), BF16),
        pltpu.VMEM((BLOCKS, T, 256), BF16),
        pltpu.VMEM((2, T, 256), F32),
        *[pltpu.VMEM((T >> l, 256), BF16) for l in (1, 2, 3)],
        pltpu.VMEM((feat, 256), BF16),
        pltpu.VMEM((feat, T), BF16),
        pltpu.VMEM((2, 128, 512), BF16),
        pltpu.VMEM((2, 128, 512), BF16),
        pltpu.VMEM((2, 128, T), BF16),
        pltpu.VMEM((272, T), BF16),
        pltpu.VMEM((LEVELS, 128, T), F32),
        pltpu.VMEM((LEVELS, 8, T), F32),
        pltpu.VMEM((T, feat), BF16),
        pltpu.VMEM((T, 256), F32),
        pltpu.VMEM((8, C, 128), F32),
        *[pltpu.VMEM((2, (1 << l) // 2, T >> l, 256), BF16) for l in (1, 2, 3)],
        *[pltpu.VMEM(((1 << l) // 2, T >> l, 256), BF16) for l in (2, 3)],
        *[pltpu.VMEM(((1 << l) // 2, T >> l, 256), BF16) for l in (2, 3)],
        *[pltpu.VMEM((max((1 << l) // 2 - 1, 1), T >> l, 256), BF16) for l in (1, 2, 3)],
        pltpu.VMEM((T // 2, 256), F32),
        *[pltpu.VMEM((COUNT[l], 256, 256), BF16) for l in (1, 2, 3)],
        dma((11,)),
        dma((11,)),
        dma((7,)),
        dma((7,)),
        dma((nh - 1,)),
        dma((nh - 1,)),
        *[dma((6,))] * 4,
        dma((5,)),
    ]
    outs = pl.pallas_call(
        functools.partial(kernel, nh),
        out_shape=(
            pltpu.VMEM((T, 256), BF16),
            pltpu.VMEM((T, 128), BF16),
            pltpu.VMEM((T, 128), BF16),
            pltpu.VMEM((T, 128), BF16),
        ),
        in_specs=[pl.BlockSpec(memory_space=pltpu.SMEM)] + [pl.BlockSpec(memory_space=pl.ANY)] * 5,
        out_specs=(vmem,) * 4,
        scratch_shapes=scratch,
        compiler_params=pltpu.CompilerParams(
            collective_id=0, has_side_effects=True, vmem_limit_bytes=56 * 1024 * 1024
        ),
        cost_estimate=pl.CostEstimate(flops=4_000_000_000, bytes_accessed=3_000_000, transcendentals=4_000_000),
    )(offsets.T, queries, key_rows, value_rows, w_out, d_out)

    anyspec = pl.BlockSpec(memory_space=pl.ANY)
    outs = [pltpu.with_memory_space_constraint(x, pltpu.VMEM) for x in outs]
    return pl.pallas_call(
        hand_out,
        out_shape=tuple(jax.ShapeDtypeStruct(x.shape, x.dtype) for x in outs),
        in_specs=[vmem] * 4,
        out_specs=(anyspec,) * 4,
        scratch_shapes=[dma((4,))],
    )(*outs)


def solution(mesh):
    in_specs = (
        P("seq", "head"),
        P("seq", "head"),
        P("seq", "head"),
        P(None, "head"),
        P("head", None),
        P("seq", "head"),
    )
    out_specs = (P("seq", "head"), P("seq", "head"), P("seq", "head"), P("seq", "head"))
    return jax.shard_map(
        functools.partial(shards, mesh.shape["head"]),
        mesh=mesh,
        in_specs=in_specs,
        out_specs=out_specs,
        check_vma=False,
    )
```
